128 devices in a mesh: dp: 8 (over y_hi, z), tensor: 16 (over y_lo, x, core).
Axes of the slice: x: 4, y: 4 (y_hi: 2, y_lo: 2; y = y_hi * 2 + y_lo), z: 4, core: 2. Of those that a mesh axis runs over, the one named last changes fastest.
Arguments:
- inputs: bfloat16 [8192, 5120], P(('dp', 'tensor')), may hold values from -24 to 24
- norm_gain: float32 [5120], replicated, may hold values from 0.5 to 1.5
- w_in: bfloat16 [5120, 20480], P(None, 'tensor'), may hold values from -0.078125 to 0.078125
- pre_gelu: bfloat16 [8192, 20480], P('dp', 'tensor'), may hold values from -6 to 6
- grad_hidden: bfloat16 [8192, 20480], P('dp', 'tensor'), may hold values from -6 to 6
- grad_out: bfloat16 [8192, 5120], P(('dp', 'tensor')), may hold values from -6 to 6
Outputs:
- grad_in: bfloat16 [8192, 5120], P(('dp', 'tensor'))
- grad_w_in: bfloat16 [5120, 20480], P('dp', 'tensor')
The draws below stay inside these ranges and needn't reach their ends.
All inputs are finite; a program needn't handle non-finite values.
Results may differ from the reference program's by a relative error of at most 0.02.
Values may be sent and summed in bfloat16 or wider, within the bound.
No kernel may reach another device: no remote copies, remote signals or barrier semaphores. Data moves between devices by JAX's collectives and lax.ppermute only.
A program may use at most 128 MiB of HBM per device.

```python
import jax
import jax.numpy as jnp
from jax import lax

D = 5120
FF = 20480
GROUP_ROWS = 1024
TOKENS = 8192
N_DP = 8
N_TENSOR = 16


def raised(result, key, source, target, parts, factor):
    owner, partner = [(jnp.arange(result.shape[dim]) // (result.shape[dim] // parts)).reshape([-1 if axis == dim else 1 for axis in range(result.ndim)]) for dim in (source, target)]
    chosen = jax.random.permutation(key, parts)[partner]
    strong = (owner == chosen) | (owner == (partner + parts // 2) % parts)
    return jnp.where(strong, factor * result, result)


def block_levels(stream_key, extent, split, smallest, top_value):
    def one(dim, parts):
        heights = jax.random.uniform(jax.random.fold_in(jax.random.fold_in(stream_key, 6), dim), (parts,), jnp.float32, smallest / len(split), top_value / len(split))
        return jnp.repeat(jnp.exp(heights), extent[dim] // parts).reshape((-1,) + (1,) * (len(extent) - dim - 1))

    level = one(*split[0])
    for cut in split[1:]:
        level = level * one(*cut)
    return level


def noise(key, extent, spread, most, cuts=(), kind=jnp.bfloat16):
    result = spread * jax.random.normal(key, extent, jnp.float32)
    if cuts:
        result = result * block_levels(key, extent, cuts, -0.22, 0.18)
    return jnp.clip(result, -most, most).astype(kind)


def gaussian_with(own_key, dims, scale, limit, pieces, heavy, dtype=jnp.bfloat16):
    drawn = scale * jax.random.normal(own_key, dims, jnp.float32)
    if pieces:
        drawn = drawn * block_levels(own_key, dims, pieces, -0.22, 0.18)
    return jnp.clip(raised(drawn, jax.random.fold_in(own_key, 3), *heavy), -limit, limit).astype(dtype)


def setup_inputs(seed: int = 0) -> dict:
    splits = jax.random.split(jax.random.key(seed), 7)
    return {
        "inputs": gaussian_with(splits[0], (TOKENS, D), 1.0, 24.0, ((0, 128),), (0, 1, 128, 5.5)),
        "norm_gain": jnp.clip(1.0 + 0.1 * jax.random.normal(splits[1], (D,), jnp.float32), 0.5, 1.5),
        "w_in": noise(splits[2], (D, FF), D ** -0.5, 0.078125, ((1, 16),)),
        "pre_gelu": noise(splits[3], (TOKENS, FF), 1.5, 6.0, ((0, 8), (1, 16))),
        "grad_hidden": noise(splits[4], (TOKENS, FF), 1.0, 6.0, ((0, 8), (1, 16))),
        "grad_out": noise(splits[5], (TOKENS, D), 1.0, 6.0, ((0, 128),)),
    }


def normalize(row_block):
    values = row_block.astype(jnp.float32)
    center = lax.optimization_barrier(jnp.mean(values, axis=1, keepdims=True))
    shifted = values - center
    variance = lax.optimization_barrier(jnp.mean(shifted * shifted, axis=1, keepdims=True))
    inv_std = lax.rsqrt(variance + 1e-05)
    return (shifted * inv_std, inv_std)

def gelu_slope(pre_vals):
    tanh_arg = 0.7978845608 * (pre_vals + 0.044715 * pre_vals * pre_vals * pre_vals)
    tangent = jnp.tanh(tanh_arg)
    return 0.5 * (1.0 + tangent) + 0.5 * pre_vals * (1.0 - tangent * tangent) * 0.7978845608 * (1.0 + 3.0 * 0.044715 * pre_vals * pre_vals)

def group_pass(row_block, pre_block, hidden_grads, out_grads, norm_gain, w_in):
    unit_rows, inv_std = normalize(row_block)
    normed = (unit_rows * norm_gain).astype(jnp.bfloat16)
    grad_pre = (hidden_grads.astype(jnp.float32) * gelu_slope(pre_block.astype(jnp.float32))).astype(jnp.bfloat16)
    part_in = lax.dot_general(normed, grad_pre, (((0,), (0,)), ((), ())), preferred_element_type=jnp.float32).astype(jnp.bfloat16)
    block_size = FF // N_TENSOR

    def add_block(block_index, running):
        offset = block_index.astype(jnp.int32) * block_size
        block_cols = lax.dynamic_slice_in_dim(grad_pre, offset, block_size, 1)
        weight_cols = lax.dynamic_slice_in_dim(w_in, offset, block_size, 1)
        block_term = lax.dot_general(block_cols, weight_cols, (((1,), (1,)), ((), ())), preferred_element_type=jnp.float32)
        return running + block_term.astype(jnp.bfloat16).astype(jnp.float32)
    grad_normed = lax.fori_loop(0, N_TENSOR, add_block, jnp.zeros(row_block.shape, jnp.float32))
    scaled = grad_normed * norm_gain
    grad_norm = inv_std * (scaled - lax.optimization_barrier(jnp.mean(scaled, axis=1, keepdims=True)) - unit_rows * lax.optimization_barrier(jnp.mean(scaled * unit_rows, axis=1, keepdims=True)))
    grad_in = (out_grads.astype(jnp.float32) + grad_norm).astype(jnp.bfloat16)
    return (grad_in, part_in)

def reference(inputs, norm_gain, w_in, pre_gelu, grad_hidden, grad_out):
    rows_all = inputs.reshape(N_DP, GROUP_ROWS, D)
    pre_all = pre_gelu.reshape(N_DP, GROUP_ROWS, FF)
    hidden_all = grad_hidden.reshape(N_DP, GROUP_ROWS, FF)
    out_all = grad_out.reshape(N_DP, GROUP_ROWS, D)

    def visit_group(running, group_data):
        grad_in, part_in = group_pass(group_data[0], group_data[1], group_data[2], group_data[3], norm_gain, w_in)
        return (running + part_in.astype(jnp.float32), grad_in)
    totals, grad_in = lax.scan(visit_group, jnp.zeros((D, FF), jnp.float32), (rows_all, pre_all, hidden_all, out_all))
    return (grad_in.reshape(TOKENS, D), totals.astype(jnp.bfloat16))
```

```python
import functools

import jax
import jax.numpy as jnp
from jax import lax
from jax.experimental import pallas as pl
from jax.experimental.pallas import tpu as pltpu
from jax.sharding import PartitionSpec as P

AXES = ("dp", "tensor")
CHUNKS = ((512, 768), (0, 512))
BF16 = jnp.bfloat16
F32 = jnp.float32
FEW = pltpu.CompilerParams(vmem_limit_bytes=16 << 20)
ROOM = pltpu.CompilerParams(vmem_limit_bytes=58 << 20)


def lasting(microseconds):
    return pl.CostEstimate(flops=int(microseconds * 0.55e9), bytes_accessed=1 << 16, transcendentals=0)


def moved(value, z=0, x=0, y=0, y_lo=0, core=0):
    pairs = []
    for source in range(128):
        yh, zz, yl, xx, cc = source // 64, source // 16 % 4, source // 8 % 2, source // 2 % 4, source % 2
        row = (yh * 2 + (yl ^ y_lo) + y) % 4
        target = ((row // 2 * 4 + (zz + z) % 4) * 2 + row % 2) * 8 + (xx + x) % 4 * 2 + (cc ^ core)
        pairs.append((source, target))
    return lax.ppermute(value, AXES, pairs)


def after(value, *others):
    return lax.optimization_barrier((value, *others))[0]


def like(*shape, kind=BF16):
    return jax.ShapeDtypeStruct(shape, kind)


def wide(ref):
    return ref[...].astype(F32)


def small(kernel, outs, *values, scratch=()):
    return pl.pallas_call(
        kernel,
        grid=(1,),
        in_specs=[pl.BlockSpec(value.shape, lambda i: (0, 0)) for value in values],
        out_specs=[pl.BlockSpec(out.shape, lambda i: (0, 0)) for out in outs],
        out_shape=outs,
        scratch_shapes=scratch,
        compiler_params=FEW,
        cost_estimate=lasting(1.2),
    )(*values)


def unit(values):
    center = jnp.mean(values, axis=1, keepdims=True)
    shifted = values - center
    inv_std = lax.rsqrt(jnp.mean(shifted * shifted, axis=1, keepdims=True) + 1e-05)
    return shifted * inv_std, inv_std


def normed_kernel(starts, rows_ref, gain_ref, *refs):
    *outs, normed = refs
    normed[...] = unit(wide(rows_ref))[0] * gain_ref[...]
    for i in range(8):
        begin = pl.multiple_of(starts[i], 128)
        outs[i // 2][:, i % 2 * 640 : i % 2 * 640 + 640] = normed[:, pl.ds(begin, 640)].astype(BF16)


def normed_blocks(starts, rows, gain):
    return pl.pallas_call(
        normed_kernel,
        grid_spec=pltpu.PrefetchScalarGridSpec(
            num_scalar_prefetch=1,
            grid=(1,),
            in_specs=[pl.BlockSpec((64, 5120), lambda i, s: (0, 0)), pl.BlockSpec((1, 5120), lambda i, s: (0, 0))],
            out_specs=[pl.BlockSpec((64, 1280), lambda i, s: (0, 0))] * 4,
            scratch_shapes=[pltpu.VMEM((64, 5120), F32)],
        ),
        out_shape=[like(64, 1280)] * 4,
        compiler_params=FEW,
        cost_estimate=lasting(1.2),
    )(starts, rows, gain)


def turn_kernel(*refs):
    rows = jnp.concatenate([wide(ref) for ref in refs[:4]], axis=0)
    refs[4][...] = rows.T.astype(BF16)


def turned(parts):
    return small(turn_kernel, [like(1280, 256)], *parts)[0]


def slope_kernel(places, pre_ref, hidden_ref, *outs):
    step = pl.program_id(0)
    for row in range(0, 256, 32):
        rows = pl.ds(row, 32)
        place = pl.multiple_of(places[4 * step + row // 64] * 64 + row % 64, 32)
        for begin in range(0, 1280, 256):
            v = pre_ref[rows, begin : begin + 256].astype(F32)
            square = v * v
            s = 1.0 / (1.0 + jnp.exp(v * (-2.0 * 0.7978845608 - (2.0 * 0.7978845608 * 0.044715) * square)))
            rate = v * (2.0 * 0.7978845608 + (6.0 * 0.7978845608 * 0.044715) * square)
            hidden = hidden_ref[rows, begin : begin + 256].astype(F32)
            grad_pre = (hidden * (s + s * (rate - rate * s))).astype(BF16)
            outs[-1][pl.ds(place, 32), begin : begin + 256] = grad_pre
            for out, (first, width) in zip(outs, CHUNKS):
                if first <= begin < first + width:
                    out[(begin - first) // 256, rows, :] = grad_pre


def grad_pre_of(places, pre_gelu, grad_hidden):
    block = pl.BlockSpec((256, 1280), lambda i, places: (i, 0))
    return pl.pallas_call(
        slope_kernel,
        grid_spec=pltpu.PrefetchScalarGridSpec(
            num_scalar_prefetch=1,
            grid=(4,),
            in_specs=[block, block],
            out_specs=[pl.BlockSpec((width // 256, 256, 256), lambda i, places: (0, i, 0)) for _, width in CHUNKS]
            + [pl.BlockSpec((1024, 1280), lambda i, places: (0, 0))],
        ),
        out_shape=[like(width // 256, 1024, 256) for _, width in CHUNKS] + [like(1024, 1280)],
        compiler_params=ROOM,
        cost_estimate=lasting(5),
    )(places, pre_gelu, grad_hidden)


def back_kernel(rows_ref, w_ref, own_ref, *far_refs):
    product = lax.dot_general(rows_ref[...], w_ref[...], (((1,), (1,)), ((), ())), preferred_element_type=F32)
    own_ref[...] = product[:512].astype(BF16)
    far_refs[0][...] = product[512:768].astype(BF16)
    far_refs[1][...] = product[768:].astype(BF16)


def back(rows, w_in, side):
    counts = (512, 256, 256)
    return pl.pallas_call(
        back_kernel,
        grid=(5,),
        in_specs=[
            pl.BlockSpec((1024, 1280), lambda i: (0, 0)),
            pl.BlockSpec((512, 1280), lambda i: (5 * side + i, 0)),
        ],
        out_specs=[pl.BlockSpec((count, 512), lambda i: (0, i)) for count in counts],
        out_shape=[like(count, 2560) for count in counts],
        compiler_params=ROOM,
        cost_estimate=lasting(1),
    )(rows, w_in)


def add_left_kernel(own_ref, *refs):
    for i in range(2):
        refs[2 + i][...] = (wide(own_ref.at[pl.ds(256 * i, 256)]) + wide(refs[i])).astype(BF16)


def add_right_kernel(own_ref, near_ref, core_ref, front_ref, rear_ref, next_ref, last_ref, keep_ref):
    def block(i, begin):
        core = (near_ref, core_ref)[i].at[pl.ds(begin, 64)]
        return (wide(own_ref.at[pl.ds(256 * i + begin, 64)]) + wide(core)).astype(BF16)

    front_ref[...] = block(0, 128)
    rear_ref[...] = block(1, 128)
    for ref, begin in ((next_ref, 64), (last_ref, 192), (keep_ref, 0)):
        ref[:64] = block(0, begin)
        ref[64:] = block(1, begin)


def added(kernel, counts, own, far):
    return pl.pallas_call(
        kernel,
        grid=(2,),
        in_specs=[pl.BlockSpec((count, 1280), lambda i: (0, i)) for count in (512, 256, 256)],
        out_specs=[pl.BlockSpec((count, 1280), lambda i: (0, i)) for count in counts],
        out_shape=[like(count, 2560) for count in counts],
        compiler_params=FEW,
        cost_estimate=lasting(1),
    )(own, *[moved(half, core=1) for half in far])


def split_left_kernel(keep_ref, other_ref, front_ref, rear_ref, next_ref, last_ref, own_ref):
    total = (wide(keep_ref) + wide(other_ref)).astype(BF16)
    own_ref[...] = total[:64]
    next_ref[...] = total[64:128]
    front_ref[...] = total[128:160]
    rear_ref[...] = total[160:192]
    last_ref[...] = total[192:]


def join_kernel(next_ref, last_ref, front_ref, rear_ref, ahead_ref, behind_ref):
    half = next_ref.shape[0] // 2
    ahead_ref[:half] = (wide(next_ref.at[:half]) + wide(front_ref)).astype(BF16)
    ahead_ref[half:] = next_ref[half:]
    behind_ref[:half] = last_ref[:half]
    behind_ref[half:] = (wide(last_ref.at[half:]) + wide(rear_ref)).astype(BF16)


def right_sum_kernel(own_ref, ahead_ref, behind_ref, keep_ref, send_ref):
    total = wide(own_ref) + wide(ahead_ref) + wide(behind_ref)
    keep_ref[...] = total[:64]
    send_ref[...] = total[64:].astype(BF16)


def end_kernel(rows_ref, gain_ref, out_grad_ref, own_ref, ahead_ref, behind_ref, keep_ref, send_ref, grad_ref, scaled):
    scaled[:, :2560] = wide(own_ref) + wide(ahead_ref) + wide(behind_ref)
    scaled[:, 2560:] = keep_ref[...] + wide(send_ref)
    unit_rows, inv_std = unit(wide(rows_ref))
    value = scaled[...] * gain_ref[...]
    mean = jnp.mean(value, axis=1, keepdims=True)
    slant = jnp.mean(value * unit_rows, axis=1, keepdims=True)
    grad_ref[...] = (wide(out_grad_ref) + inv_std * (value - mean - unit_rows * slant)).astype(BF16)


def add_halves(out_ref, value, up_ref, down_ref):
    out_ref[:320] = (value[:320].astype(F32) + up_ref[0].astype(F32)).astype(BF16)
    out_ref[320:] = (value[320:].astype(F32) + down_ref[0].astype(F32)).astype(BF16)


def weight_kernel(task, columns_ref, *refs):
    pieces, refs = refs[:4], refs[4:]
    total = None
    for begin in range(0, 16, 4):
        blocks = range(begin, begin + 4)
        left = jnp.concatenate([columns_ref[b] for b in blocks], axis=1)
        right = jnp.concatenate([piece[0, b * 64 : b * 64 + 64, :] for b in blocks for piece in pieces], axis=0)
        term = jnp.dot(left, right, preferred_element_type=F32)
        total = term if total is None else total + term
    if task == "send":
        refs[0][0] = total[:320].astype(BF16)
        refs[1][0] = total[320:].astype(BF16)
    elif task == "keep":
        refs[0][0] = total.astype(BF16)
    else:
        add_halves(refs[2], total, refs[0], refs[1])


def weight(task, columns, pieces, other=()):
    steps = pieces[0].shape[0]
    half = pl.BlockSpec((1, 320, 256), lambda i: (i, 0, 0))
    if task == "send":
        outs, shapes = [half, half], [like(steps, 320, 256)] * 2
    elif task == "keep":
        outs, shapes = [pl.BlockSpec((1, 640, 256), lambda i: (i, 0, 0))], [like(steps, 640, 256)]
    else:
        outs, shapes = [pl.BlockSpec((640, 256), lambda i: (0, 2 + i))], [like(640, 1280)]
    return pl.pallas_call(
        functools.partial(weight_kernel, task),
        grid=(steps,),
        in_specs=[pl.BlockSpec((16, 640, 256), lambda i: (0, int(task == "send"), 0))]
        + [pl.BlockSpec((1, 1024, 256), lambda i: (i, 0, 0))] * 4
        + [half] * len(other),
        out_specs=outs,
        out_shape=shapes,
        compiler_params=ROOM,
        cost_estimate=lasting(1.5 + 1.8 * steps),
    )(columns, *pieces, *other)


def put_kernel(keep_ref, up_ref, down_ref, given_ref, out_ref):
    add_halves(out_ref, keep_ref[0], up_ref, down_ref)


def put(keep, up, down, given):
    half = pl.BlockSpec((1, 320, 256), lambda i: (i, 0, 0))
    return pl.pallas_call(
        put_kernel,
        grid=(2,),
        in_specs=[pl.BlockSpec((1, 640, 256), lambda i: (i, 0, 0)), half, half, pl.BlockSpec(memory_space=pl.ANY)],
        out_specs=pl.BlockSpec((640, 256), lambda i: (0, i)),
        out_shape=like(640, 1280),
        input_output_aliases={3: 0},
        compiler_params=ROOM,
        cost_estimate=lasting(2),
    )(keep, up, down, given)


def local(inputs, norm_gain, w_in, pre_gelu, grad_hidden, grad_out):
    group, place = lax.axis_index("dp"), lax.axis_index("tensor")
    y_hi, z = group // 4, group % 4
    y_lo, x, core = place // 8, place // 2 % 4, place % 2
    gain = norm_gain.reshape(1, 5120)

    step = jnp.arange(8, dtype=jnp.int32)
    starts = (((y_hi ^ (step % 2)) * 4 + (z + step // 2) % 4) * 640).astype(jnp.int32)
    block = jnp.arange(16, dtype=jnp.int32)
    places = ((core ^ (block % 2)) * 8 + (y_lo ^ (block // 8)) * 4 + (block // 2 % 4 - x + 4) % 4).astype(jnp.int32)

    blocks = normed_blocks(starts, inputs, gain)
    parts = [blocks[0], moved(blocks[3], z=-1), moved(blocks[2], z=2), moved(blocks[1], z=1)]
    *chunks, rows = grad_pre_of(after(places, *blocks), pre_gelu, grad_hidden)
    one = turned([after(parts[0], rows), *parts[1:]])
    columns = lax.all_gather(one, "tensor", axis=0, tiled=False)

    first = [moved(chunks[0], z=-1), moved(chunks[0], z=1)]

    own_right, *far_right = back(after(rows, one), w_in, 1)
    own_left, *far_left = back(after(rows, own_right), w_in, 0)
    own_right = after(own_right, own_left, *first)
    front, rear, next_right, last_right, own_right = added(
        add_right_kernel, [64, 64, 128, 128, 128], own_right, far_right
    )
    front, rear = moved(front, x=1), moved(rear, x=-1)
    keep, send = added(add_left_kernel, [256, 256], after(own_left, own_right), far_left)
    send = moved(send, y_lo=1)

    first_far = moved(first[1], z=1)
    second_next = moved(after(chunks[1], *first), z=-1)
    ahead, behind = small(join_kernel, [like(128, 2560)] * 2, next_right, last_right, front, rear)
    second_far = moved(after(second_next, ahead), z=-1)
    second_last = moved(after(chunks[1], second_next, ahead), z=1)
    pieces = [[chunks[0], first[0], first_far, first[1]], [chunks[1], second_next, second_far, second_last]]
    ahead, behind = moved(ahead, x=1), moved(behind, x=-1)

    sent = weight("send", after(columns, second_next, ahead, behind), pieces[0])
    hop = [moved(sent[0], y=1), moved(sent[1], y=-1)]
    other = [moved(hop[0], y=1), moved(hop[1], y=-1)]

    right_keep, right_send = small(
        right_sum_kernel, [like(64, 2560, kind=F32), like(64, 2560)], after(own_right, *sent), ahead, behind
    )
    right_send = moved(right_send, y_lo=1)
    outs = [like(count, 2560) for count in (32, 32, 64, 64, 64)]
    keep = after(keep, *sent)
    front, rear, next_left, last_left, own_left = small(split_left_kernel, outs, keep, send)
    front, rear = moved(front, x=1), moved(rear, x=-1)
    sides = small(join_kernel, [like(64, 2560)] * 2, next_left, last_left, front, rear)
    ahead, behind = moved(sides[0], x=1), moved(sides[1], x=-1)

    sent = weight("send", after(columns, right_keep, *sides, *hop), pieces[1])
    hop = [moved(sent[0], y=1), moved(sent[1], y=-1)]
    (kept,) = weight("keep", after(columns, *sent), pieces[1])
    (grad_w_in,) = weight("put", after(columns, kept), pieces[0], other)
    (grad_in,) = small(
        end_kernel,
        [like(64, 5120)],
        inputs,
        gain,
        grad_out,
        after(own_left, grad_w_in),
        ahead,
        behind,
        right_keep,
        right_send,
        scratch=[pltpu.VMEM((64, 5120), F32)],
    )
    grad_w_in = put(after(kept, grad_in), moved(hop[0], y=1), moved(hop[1], y=-1), grad_w_in)
    return (grad_in, grad_w_in)


def solution(mesh):
    placed = (
        P(("dp", "tensor"), None),
        P(),
        P(None, "tensor"),
        P("dp", "tensor"),
        P("dp", "tensor"),
        P(("dp", "tensor"), None),
    )
    return jax.shard_map(
        local,
        mesh=mesh,
        in_specs=placed,
        out_specs=(P(("dp", "tensor"), None), P("dp", "tensor")),
        check_vma=False,
    )
```

```python
import functools

import jax
import jax.numpy as jnp
from jax import lax
from jax.experimental import pallas as pl
from jax.experimental.pallas import tpu as pltpu
from jax.sharding import PartitionSpec as P

AXES = ("dp", "tensor")
CHUNKS = ((512, 768), (0, 512))
BF16 = jnp.bfloat16
F32 = jnp.float32
FEW = pltpu.CompilerParams(vmem_limit_bytes=16 << 20)
ROOM = pltpu.CompilerParams(vmem_limit_bytes=58 << 20)


def lasting(microseconds):
    return pl.CostEstimate(flops=int(microseconds * 0.55e9), bytes_accessed=1 << 16, transcendentals=0)


def moved(value, z=0, x=0, y=0, y_lo=0, core=0):
    pairs = []
    for source in range(128):
        yh, zz, yl, xx, cc = source // 64, source // 16 % 4, source // 8 % 2, source // 2 % 4, source % 2
        row = (yh * 2 + (yl ^ y_lo) + y) % 4
        target = ((row // 2 * 4 + (zz + z) % 4) * 2 + row % 2) * 8 + (xx + x) % 4 * 2 + (cc ^ core)
        pairs.append((source, target))
    return lax.ppermute(value, AXES, pairs)


def after(value, *others):
    return lax.optimization_barrier((value, *others))[0]


def like(*shape, kind=BF16):
    return jax.ShapeDtypeStruct(shape, kind)


def wide(ref):
    return ref[...].astype(F32)


def small(kernel, outs, *values, scratch=(), lasts=1.2):
    return pl.pallas_call(
        kernel,
        grid=(1,),
        in_specs=[pl.BlockSpec(value.shape, lambda i: (0, 0)) for value in values],
        out_specs=[pl.BlockSpec(out.shape, lambda i: (0, 0)) for out in outs],
        out_shape=outs,
        scratch_shapes=scratch,
        compiler_params=FEW,
        cost_estimate=lasting(lasts),
    )(*values)


def unit(values):
    center = jnp.mean(values, axis=1, keepdims=True)
    shifted = values - center
    inv_std = lax.rsqrt(jnp.mean(shifted * shifted, axis=1, keepdims=True) + 1e-05)
    return shifted * inv_std, inv_std


def normed_kernel(starts, rows_ref, gain_ref, *refs):
    *outs, normed = refs
    normed[...] = unit(wide(rows_ref))[0] * gain_ref[...]
    for i in range(8):
        begin = pl.multiple_of(starts[i], 128)
        outs[i // 2][:, i % 2 * 640 : i % 2 * 640 + 640] = normed[:, pl.ds(begin, 640)].astype(BF16)


def normed_blocks(starts, rows, gain):
    return pl.pallas_call(
        normed_kernel,
        grid_spec=pltpu.PrefetchScalarGridSpec(
            num_scalar_prefetch=1,
            grid=(1,),
            in_specs=[pl.BlockSpec((64, 5120), lambda i, s: (0, 0)), pl.BlockSpec((1, 5120), lambda i, s: (0, 0))],
            out_specs=[pl.BlockSpec((64, 1280), lambda i, s: (0, 0))] * 4,
            scratch_shapes=[pltpu.VMEM((64, 5120), F32)],
        ),
        out_shape=[like(64, 1280)] * 4,
        compiler_params=ROOM,
        cost_estimate=lasting(1.2),
    )(starts, rows, gain)


def turn_kernel(*refs):
    rows = jnp.concatenate([wide(ref) for ref in refs[:4]], axis=0)
    refs[4][...] = rows.T.astype(BF16)


def turned(parts):
    return small(turn_kernel, [like(1280, 256)], *parts)[0]


def slope_kernel(places, pre_ref, hidden_ref, *outs):
    step = pl.program_id(0)
    for row in range(0, 256, 32):
        rows = pl.ds(row, 32)
        place = pl.multiple_of(places[4 * step + row // 64] * 64 + row % 64, 32)
        for begin in range(0, 1280, 256):
            v = pre_ref[rows, begin : begin + 256].astype(F32)
            square = v * v
            s = 1.0 / (1.0 + jnp.exp(v * (-2.0 * 0.7978845608 - (2.0 * 0.7978845608 * 0.044715) * square)))
            rate = v * (2.0 * 0.7978845608 + (6.0 * 0.7978845608 * 0.044715) * square)
            hidden = hidden_ref[rows, begin : begin + 256].astype(F32)
            grad_pre = (hidden * (s + s * (rate - rate * s))).astype(BF16)
            outs[-1][pl.ds(place, 32), begin : begin + 256] = grad_pre
            for out, (first, width) in zip(outs, CHUNKS):
                if first <= begin < first + width:
                    out[(begin - first) // 256, rows, :] = grad_pre


def grad_pre_of(places, pre_gelu, grad_hidden):
    block = pl.BlockSpec((256, 1280), lambda i, places: (i, 0))
    return pl.pallas_call(
        slope_kernel,
        grid_spec=pltpu.PrefetchScalarGridSpec(
            num_scalar_prefetch=1,
            grid=(4,),
            in_specs=[block, block],
            out_specs=[pl.BlockSpec((width // 256, 256, 256), lambda i, places: (0, i, 0)) for _, width in CHUNKS]
            + [pl.BlockSpec((1024, 1280), lambda i, places: (0, 0))],
        ),
        out_shape=[like(width // 256, 1024, 256) for _, width in CHUNKS] + [like(1024, 1280)],
        compiler_params=ROOM,
        cost_estimate=lasting(5),
    )(places, pre_gelu, grad_hidden)


def back_kernel(rows_ref, w_ref, own_ref, *far_refs):
    product = lax.dot_general(rows_ref[...], w_ref[...], (((1,), (1,)), ((), ())), preferred_element_type=F32)
    own_ref[...] = product[:512].astype(BF16)
    far_refs[0][...] = product[512:768].astype(BF16)
    far_refs[1][...] = product[768:].astype(BF16)


def back(rows, w_in, side):
    counts = (512, 256, 256)
    return pl.pallas_call(
        back_kernel,
        grid=(5,),
        in_specs=[
            pl.BlockSpec((1024, 1280), lambda i: (0, 0)),
            pl.BlockSpec((512, 1280), lambda i: (5 * side + i, 0)),
        ],
        out_specs=[pl.BlockSpec((count, 512), lambda i: (0, i)) for count in counts],
        out_shape=[like(count, 2560) for count in counts],
        compiler_params=ROOM,
        cost_estimate=lasting(1),
    )(rows, w_in)


def add_left_kernel(own_ref, *refs):
    for i in range(2):
        refs[2 + i][...] = (wide(own_ref.at[pl.ds(256 * i, 256)]) + wide(refs[i])).astype(BF16)


def add_right_kernel(own_ref, near_ref, core_ref, front_ref, rear_ref, next_ref, last_ref, keep_ref):
    def block(i, begin):
        core = (near_ref, core_ref)[i].at[pl.ds(begin, 64)]
        return (wide(own_ref.at[pl.ds(256 * i + begin, 64)]) + wide(core)).astype(BF16)

    front_ref[...] = block(0, 128)
    rear_ref[...] = block(1, 128)
    for ref, begin in ((next_ref, 64), (last_ref, 192), (keep_ref, 0)):
        ref[:64] = block(0, begin)
        ref[64:] = block(1, begin)


def added(kernel, counts, own, far):
    return pl.pallas_call(
        kernel,
        grid=(2,),
        in_specs=[pl.BlockSpec((count, 1280), lambda i: (0, i)) for count in (512, 256, 256)],
        out_specs=[pl.BlockSpec((count, 1280), lambda i: (0, i)) for count in counts],
        out_shape=[like(count, 2560) for count in counts],
        compiler_params=FEW,
        cost_estimate=lasting(1),
    )(own, *[moved(half, core=1) for half in far])


def split_left_kernel(keep_ref, other_ref, front_ref, rear_ref, next_ref, last_ref, own_ref):
    total = (wide(keep_ref) + wide(other_ref)).astype(BF16)
    own_ref[...] = total[:64]
    next_ref[...] = total[64:128]
    front_ref[...] = total[128:160]
    rear_ref[...] = total[160:192]
    last_ref[...] = total[192:]


def join_kernel(next_ref, last_ref, front_ref, rear_ref, ahead_ref, behind_ref):
    half = next_ref.shape[0] // 2
    ahead_ref[:half] = (wide(next_ref.at[:half]) + wide(front_ref)).astype(BF16)
    ahead_ref[half:] = next_ref[half:]
    behind_ref[:half] = last_ref[:half]
    behind_ref[half:] = (wide(last_ref.at[half:]) + wide(rear_ref)).astype(BF16)


def right_sum_kernel(own_ref, ahead_ref, behind_ref, keep_ref, send_ref):
    total = wide(own_ref) + wide(ahead_ref) + wide(behind_ref)
    keep_ref[...] = total[:64]
    send_ref[...] = total[64:].astype(BF16)


def end_kernel(rows_ref, gain_ref, out_grad_ref, own_ref, ahead_ref, behind_ref, keep_ref, send_ref, grad_ref, scaled):
    scaled[:, :2560] = wide(own_ref) + wide(ahead_ref) + wide(behind_ref)
    scaled[:, 2560:] = keep_ref[...] + wide(send_ref)
    unit_rows, inv_std = unit(wide(rows_ref))
    value = scaled[...] * gain_ref[...]
    mean = jnp.mean(value, axis=1, keepdims=True)
    slant = jnp.mean(value * unit_rows, axis=1, keepdims=True)
    grad_ref[...] = (wide(out_grad_ref) + inv_std * (value - mean - unit_rows * slant)).astype(BF16)


def add_halves(out_ref, value, up_ref, down_ref):
    out_ref[:320] = (value[:320].astype(F32) + up_ref[0].astype(F32)).astype(BF16)
    out_ref[320:] = (value[320:].astype(F32) + down_ref[0].astype(F32)).astype(BF16)


def weight_kernel(task, columns_ref, *refs):
    pieces, refs = refs[:4], refs[4:]
    total = None
    for begin in range(0, 16, 4):
        blocks = range(begin, begin + 4)
        left = jnp.concatenate([columns_ref[b] for b in blocks], axis=1)
        right = jnp.concatenate([piece[0, b * 64 : b * 64 + 64, :] for b in blocks for piece in pieces], axis=0)
        term = jnp.dot(left, right, preferred_element_type=F32)
        total = term if total is None else total + term
    if task != "send":
        refs[0][0] = total[:640].astype(BF16)
    if task != "keep":
        rows = total.shape[0]
        refs[-2][0] = total[rows - 640 : rows - 320].astype(BF16)
        refs[-1][0] = total[rows - 320 :].astype(BF16)


def weight(task, columns, pieces):
    steps = pieces[0].shape[0]
    half = pl.BlockSpec((1, 320, 256), lambda i: (i, 0, 0))
    taken = pl.BlockSpec((16, 640, 256), lambda i: (0, int(task == "send"), 0))
    if task == "both":
        taken = pl.BlockSpec((16, 1280, 256), lambda i: (0, 0, 0))
    outs, shapes = [], []
    if task != "send":
        outs, shapes = [pl.BlockSpec((1, 640, 256), lambda i: (i, 0, 0))], [like(steps, 640, 256)]
    if task != "keep":
        outs, shapes = outs + [half, half], shapes + [like(steps, 320, 256)] * 2
    return pl.pallas_call(
        functools.partial(weight_kernel, task),
        grid=(steps,),
        in_specs=[taken]
        + [pl.BlockSpec((1, 1024, 256), lambda i: (i, 0, 0))] * 4,
        out_specs=outs,
        out_shape=shapes,
        compiler_params=ROOM,
        cost_estimate=lasting(1.5 + 1.8 * steps),
    )(columns, *pieces)


def put_kernel(keep_ref, up_ref, down_ref, *refs):
    add_halves(refs[-1], keep_ref[0], up_ref, down_ref)


def put(keep, up, down, place, given=()):
    half = pl.BlockSpec((1, 320, 256), lambda i: (i, 0, 0))
    return pl.pallas_call(
        put_kernel,
        grid=(keep.shape[0],),
        in_specs=[pl.BlockSpec((1, 640, 256), lambda i: (i, 0, 0)), half, half]
        + [pl.BlockSpec(memory_space=pl.ANY)] * len(given),
        out_specs=pl.BlockSpec((640, 256), lambda i: (0, place + i)),
        out_shape=like(640, 1280),
        input_output_aliases={3: 0} if given else {},
        compiler_params=FEW,
        cost_estimate=lasting(2),
    )(keep, up, down, *given)


def local(inputs, norm_gain, w_in, pre_gelu, grad_hidden, grad_out):
    group, place = lax.axis_index("dp"), lax.axis_index("tensor")
    y_hi, z = group // 4, group % 4
    y_lo, x, core = place // 8, place // 2 % 4, place % 2
    gain = norm_gain.reshape(1, 5120)

    step = jnp.arange(8, dtype=jnp.int32)
    starts = (((y_hi ^ (step % 2)) * 4 + (z + step // 2) % 4) * 640).astype(jnp.int32)
    block = jnp.arange(16, dtype=jnp.int32)
    places = ((core ^ (block % 2)) * 8 + (y_lo ^ (block // 8)) * 4 + (block // 2 % 4 - x + 4) % 4).astype(jnp.int32)

    blocks = normed_blocks(starts, inputs, gain)
    parts = [blocks[0], moved(blocks[3], z=-1), moved(blocks[2], z=2), moved(blocks[1], z=1)]
    *chunks, rows = grad_pre_of(after(places, *blocks), pre_gelu, grad_hidden)
    one = turned([after(parts[0], rows), *parts[1:]])
    columns = lax.all_gather(one, "tensor", axis=0, tiled=False)

    first = [moved(chunks[0], z=-1), moved(chunks[0], z=1)]

    own_right, *far_right = back(after(rows, one), w_in, 1)
    own_left, *far_left = back(after(rows, own_right), w_in, 0)
    own_right = after(own_right, own_left, *first)
    front, rear, next_right, last_right, own_right = added(
        add_right_kernel, [64, 64, 128, 128, 128], own_right, far_right
    )
    front, rear = moved(front, x=1), moved(rear, x=-1)
    keep, send = added(add_left_kernel, [256, 256], after(own_left, own_right), far_left)
    send = moved(send, y_lo=1)

    first_far = moved(after(first[1], own_right), z=1)
    second_next = moved(after(chunks[1], *first, own_right), z=-1)
    next_right = after(next_right, keep)
    ahead, behind = small(join_kernel, [like(128, 2560)] * 2, next_right, last_right, front, rear, lasts=1.2)
    second_far = moved(after(second_next, ahead), z=-1)
    second_last = moved(after(chunks[1], second_next, ahead, first_far), z=1)
    pieces = [[chunks[0], first[0], first_far, first[1]], [chunks[1], second_next, second_far, second_last]]
    ahead, behind = moved(ahead, x=1), moved(behind, x=-1)

    kept, *sent = weight("both", after(columns, second_next, ahead, behind), pieces[0])
    hop = [moved(sent[0], y=1), moved(sent[1], y=-1)]

    outs = [like(count, 2560) for count in (32, 32, 64, 64, 64)]
    keep = after(keep, *sent, second_far)
    front, rear, next_left, last_left, own_left = small(split_left_kernel, outs, keep, send)
    front, rear = moved(front, x=1), moved(rear, x=-1)

    kept_1, *sent = weight("both", after(columns, own_left), pieces[1])
    other = [moved(after(rows, kept_1), y=way) for rows, way in zip(hop, (1, -1))]
    next_left = after(next_left, *sent)
    sides = small(join_kernel, [like(64, 2560)] * 2, next_left, last_left, front, rear)
    right_keep, right_send = small(
        right_sum_kernel, [like(64, 2560, kind=F32), like(64, 2560)], after(own_right, *sent), ahead, behind
    )
    right_send = moved(right_send, y_lo=1)
    ahead, behind = moved(sides[0], x=1), moved(sides[1], x=-1)
    hop = [moved(sent[0], y=1), moved(sent[1], y=-1)]
    grad_w_in = put(after(kept, kept_1), *other, 2)
    (grad_in,) = small(
        end_kernel,
        [like(64, 5120)],
        inputs,
        gain,
        grad_out,
        after(own_left, grad_w_in),
        ahead,
        behind,
        right_keep,
        right_send,
        scratch=[pltpu.VMEM((64, 5120), F32)],
    )
    grad_w_in = put(after(kept_1, grad_in), moved(hop[0], y=1), moved(hop[1], y=-1), 0, [grad_w_in])
    return (grad_in, grad_w_in)


def solution(mesh):
    placed = (
        P(("dp", "tensor"), None),
        P(),
        P(None, "tensor"),
        P("dp", "tensor"),
        P("dp", "tensor"),
        P(("dp", "tensor"), None),
    )
    return jax.shard_map(
        local,
        mesh=mesh,
        in_specs=placed,
        out_specs=(P(("dp", "tensor"), None), P("dp", "tensor")),
        check_vma=False,
    )
```

```python
import functools

import jax
import jax.numpy as jnp
from jax import lax
from jax.experimental import pallas as pl
from jax.experimental.pallas import tpu as pltpu
from jax.sharding import PartitionSpec as P

AXES = ("dp", "tensor")
CHUNKS = ((512, 768), (0, 512))
BF16 = jnp.bfloat16
F32 = jnp.float32
FEW = pltpu.CompilerParams(vmem_limit_bytes=16 << 20)
ROOM = pltpu.CompilerParams(vmem_limit_bytes=58 << 20)


def lasting(microseconds):
    return pl.CostEstimate(flops=int(microseconds * 0.55e9), bytes_accessed=1 << 16, transcendentals=0)


def moved(value, z=0, x=0, y=0, y_lo=0, core=0):
    pairs = []
    for source in range(128):
        yh, zz, yl, xx, cc = source // 64, source // 16 % 4, source // 8 % 2, source // 2 % 4, source % 2
        row = (yh * 2 + (yl ^ y_lo) + y) % 4
        target = ((row // 2 * 4 + (zz + z) % 4) * 2 + row % 2) * 8 + (xx + x) % 4 * 2 + (cc ^ core)
        pairs.append((source, target))
    return lax.ppermute(value, AXES, pairs)


def after(value, *others):
    return lax.optimization_barrier((value, *others))[0]


def like(*shape, kind=BF16):
    return jax.ShapeDtypeStruct(shape, kind)


def wide(ref):
    return ref[...].astype(F32)


def small(kernel, outs, *values, scratch=(), lasts=1.2):
    return pl.pallas_call(
        kernel,
        grid=(1,),
        in_specs=[pl.BlockSpec(value.shape, lambda i: (0, 0)) for value in values],
        out_specs=[pl.BlockSpec(out.shape, lambda i: (0, 0)) for out in outs],
        out_shape=outs,
        scratch_shapes=scratch,
        compiler_params=FEW,
        cost_estimate=lasting(lasts),
    )(*values)


def unit(values):
    center = jnp.mean(values, axis=1, keepdims=True)
    shifted = values - center
    inv_std = lax.rsqrt(jnp.mean(shifted * shifted, axis=1, keepdims=True) + 1e-05)
    return shifted * inv_std, inv_std


def normed_kernel(starts, rows_ref, gain_ref, *refs):
    *outs, normed = refs
    normed[...] = unit(wide(rows_ref))[0] * gain_ref[...]
    for i in range(8):
        begin = pl.multiple_of(starts[i], 128)
        outs[i // 2][:, i % 2 * 640 : i % 2 * 640 + 640] = normed[:, pl.ds(begin, 640)].astype(BF16)


def normed_blocks(starts, rows, gain):
    return pl.pallas_call(
        normed_kernel,
        grid_spec=pltpu.PrefetchScalarGridSpec(
            num_scalar_prefetch=1,
            grid=(1,),
            in_specs=[pl.BlockSpec((64, 5120), lambda i, s: (0, 0)), pl.BlockSpec((1, 5120), lambda i, s: (0, 0))],
            out_specs=[pl.BlockSpec((64, 1280), lambda i, s: (0, 0))] * 4,
            scratch_shapes=[pltpu.VMEM((64, 5120), F32)],
        ),
        out_shape=[like(64, 1280)] * 4,
        compiler_params=ROOM,
        cost_estimate=lasting(1.2),
    )(starts, rows, gain)


def turn_kernel(*refs):
    rows = jnp.concatenate([wide(ref) for ref in refs[:4]], axis=0)
    refs[4][...] = rows.T.astype(BF16)


def turned(parts):
    return small(turn_kernel, [like(1280, 256)], *parts)[0]


def slope_kernel(places, pre_ref, hidden_ref, *outs):
    step = pl.program_id(0)
    for row in range(0, 256, 32):
        rows = pl.ds(row, 32)
        place = pl.multiple_of(places[4 * step + row // 64] * 64 + row % 64, 32)
        for begin in range(0, 1280, 256):
            v = pre_ref[rows, begin : begin + 256].astype(F32)
            square = v * v
            s = 1.0 / (1.0 + jnp.exp(v * (-2.0 * 0.7978845608 - (2.0 * 0.7978845608 * 0.044715) * square)))
            rate = v * (2.0 * 0.7978845608 + (6.0 * 0.7978845608 * 0.044715) * square)
            hidden = hidden_ref[rows, begin : begin + 256].astype(F32)
            grad_pre = (hidden * (s + s * (rate - rate * s))).astype(BF16)
            outs[-1][pl.ds(place, 32), begin : begin + 256] = grad_pre
            for out, (first, width) in zip(outs, CHUNKS):
                if first <= begin < first + width:
                    out[(begin - first) // 256, rows, :] = grad_pre


def grad_pre_of(places, pre_gelu, grad_hidden):
    block = pl.BlockSpec((256, 1280), lambda i, places: (i, 0))
    return pl.pallas_call(
        slope_kernel,
        grid_spec=pltpu.PrefetchScalarGridSpec(
            num_scalar_prefetch=1,
            grid=(4,),
            in_specs=[block, block],
            out_specs=[pl.BlockSpec((width // 256, 256, 256), lambda i, places: (0, i, 0)) for _, width in CHUNKS]
            + [pl.BlockSpec((1024, 1280), lambda i, places: (0, 0))],
        ),
        out_shape=[like(width // 256, 1024, 256) for _, width in CHUNKS] + [like(1024, 1280)],
        compiler_params=ROOM,
        cost_estimate=lasting(5),
    )(places, pre_gelu, grad_hidden)


def back_kernel(rows_ref, w_ref, own_ref, *far_refs):
    product = lax.dot_general(rows_ref[...], w_ref[...], (((1,), (1,)), ((), ())), preferred_element_type=F32)
    own_ref[...] = product[:512].astype(BF16)
    far_refs[0][...] = product[512:768].astype(BF16)
    far_refs[1][...] = product[768:].astype(BF16)


def back(rows, w_in, side):
    counts = (512, 256, 256)
    return pl.pallas_call(
        back_kernel,
        grid=(5,),
        in_specs=[
            pl.BlockSpec((1024, 1280), lambda i: (0, 0)),
            pl.BlockSpec((512, 1280), lambda i: (5 * side + i, 0)),
        ],
        out_specs=[pl.BlockSpec((count, 512), lambda i: (0, i)) for count in counts],
        out_shape=[like(count, 2560) for count in counts],
        compiler_params=ROOM,
        cost_estimate=lasting(1),
    )(rows, w_in)


def add_left_kernel(own_ref, *refs):
    for i in range(2):
        refs[2 + i][...] = (wide(own_ref.at[pl.ds(256 * i, 256)]) + wide(refs[i])).astype(BF16)


def add_right_kernel(own_ref, near_ref, core_ref, front_ref, rear_ref, next_ref, last_ref, keep_ref):
    def block(i, begin):
        core = (near_ref, core_ref)[i].at[pl.ds(begin, 64)]
        return (wide(own_ref.at[pl.ds(256 * i + begin, 64)]) + wide(core)).astype(BF16)

    front_ref[...] = block(0, 128)
    rear_ref[...] = block(1, 128)
    for ref, begin in ((next_ref, 64), (last_ref, 192), (keep_ref, 0)):
        ref[:64] = block(0, begin)
        ref[64:] = block(1, begin)


def added(kernel, counts, own, far):
    return pl.pallas_call(
        kernel,
        grid=(2,),
        in_specs=[pl.BlockSpec((count, 1280), lambda i: (0, i)) for count in (512, 256, 256)],
        out_specs=[pl.BlockSpec((count, 1280), lambda i: (0, i)) for count in counts],
        out_shape=[like(count, 2560) for count in counts],
        compiler_params=FEW,
        cost_estimate=lasting(1),
    )(own, *[moved(half, core=1) for half in far])


def split_left_kernel(keep_ref, other_ref, front_ref, rear_ref, next_ref, last_ref, own_ref):
    total = (wide(keep_ref) + wide(other_ref)).astype(BF16)
    own_ref[...] = total[:64]
    next_ref[...] = total[64:128]
    front_ref[...] = total[128:160]
    rear_ref[...] = total[160:192]
    last_ref[...] = total[192:]


def join_kernel(next_ref, last_ref, front_ref, rear_ref, ahead_ref, behind_ref):
    half = next_ref.shape[0] // 2
    ahead_ref[:half] = (wide(next_ref.at[:half]) + wide(front_ref)).astype(BF16)
    ahead_ref[half:] = next_ref[half:]
    behind_ref[:half] = last_ref[:half]
    behind_ref[half:] = (wide(last_ref.at[half:]) + wide(rear_ref)).astype(BF16)


def right_sum_kernel(own_ref, ahead_ref, behind_ref, keep_ref, send_ref):
    total = wide(own_ref) + wide(ahead_ref) + wide(behind_ref)
    keep_ref[...] = total[:64]
    send_ref[...] = total[64:].astype(BF16)


def end_kernel(rows_ref, gain_ref, out_grad_ref, own_ref, ahead_ref, behind_ref, keep_ref, send_ref, grad_ref, scaled):
    scaled[:, :2560] = wide(own_ref) + wide(ahead_ref) + wide(behind_ref)
    scaled[:, 2560:] = keep_ref[...] + wide(send_ref)
    unit_rows, inv_std = unit(wide(rows_ref))
    value = scaled[...] * gain_ref[...]
    mean = jnp.mean(value, axis=1, keepdims=True)
    slant = jnp.mean(value * unit_rows, axis=1, keepdims=True)
    grad_ref[...] = (wide(out_grad_ref) + inv_std * (value - mean - unit_rows * slant)).astype(BF16)


def add_halves(out_ref, value, up_ref, down_ref):
    out_ref[:320] = (value[:320].astype(F32) + up_ref[0].astype(F32)).astype(BF16)
    out_ref[320:] = (value[320:].astype(F32) + down_ref[0].astype(F32)).astype(BF16)


def weight_kernel(task, columns_ref, *refs):
    pieces, refs = refs[:4], refs[4:]
    total = None
    for begin in range(0, 16, 4):
        blocks = range(begin, begin + 4)
        left = jnp.concatenate([columns_ref[b] for b in blocks], axis=1)
        right = jnp.concatenate([piece[0, b * 64 : b * 64 + 64, :] for b in blocks for piece in pieces], axis=0)
        term = jnp.dot(left, right, preferred_element_type=F32)
        total = term if total is None else total + term
    if task != "send":
        refs[0][0] = total[:640].astype(BF16)
    if task != "keep":
        rows = total.shape[0]
        refs[-2][0] = total[rows - 640 : rows - 320].astype(BF16)
        refs[-1][0] = total[rows - 320 :].astype(BF16)


def weight(task, columns, pieces):
    steps = pieces[0].shape[0]
    half = pl.BlockSpec((1, 320, 256), lambda i: (i, 0, 0))
    taken = pl.BlockSpec((16, 640, 256), lambda i: (0, int(task == "send"), 0))
    if task == "both":
        taken = pl.BlockSpec((16, 1280, 256), lambda i: (0, 0, 0))
    outs, shapes = [], []
    if task != "send":
        outs, shapes = [pl.BlockSpec((1, 640, 256), lambda i: (i, 0, 0))], [like(steps, 640, 256)]
    if task != "keep":
        outs, shapes = outs + [half, half], shapes + [like(steps, 320, 256)] * 2
    return pl.pallas_call(
        functools.partial(weight_kernel, task),
        grid=(steps,),
        in_specs=[taken]
        + [pl.BlockSpec((1, 1024, 256), lambda i: (i, 0, 0))] * 4,
        out_specs=outs,
        out_shape=shapes,
        compiler_params=ROOM,
        cost_estimate=lasting(2 + 2.4 * steps),
    )(columns, *pieces)


def put_kernel(keep_ref, up_ref, down_ref, *refs):
    add_halves(refs[-1], keep_ref[0], up_ref, down_ref)


def put(keep, up, down, place, given=()):
    half = pl.BlockSpec((1, 320, 256), lambda i: (i, 0, 0))
    return pl.pallas_call(
        put_kernel,
        grid=(keep.shape[0],),
        in_specs=[pl.BlockSpec((1, 640, 256), lambda i: (i, 0, 0)), half, half]
        + [pl.BlockSpec(memory_space=pl.ANY)] * len(given),
        out_specs=pl.BlockSpec((640, 256), lambda i: (0, place + i)),
        out_shape=like(640, 1280),
        input_output_aliases={3: 0} if given else {},
        compiler_params=FEW,
        cost_estimate=lasting(2),
    )(keep, up, down, *given)


def local(inputs, norm_gain, w_in, pre_gelu, grad_hidden, grad_out):
    group, place = lax.axis_index("dp"), lax.axis_index("tensor")
    y_hi, z = group // 4, group % 4
    y_lo, x, core = place // 8, place // 2 % 4, place % 2
    gain = norm_gain.reshape(1, 5120)

    step = jnp.arange(8, dtype=jnp.int32)
    starts = (((y_hi ^ (step % 2)) * 4 + (z + step // 2) % 4) * 640).astype(jnp.int32)
    block = jnp.arange(16, dtype=jnp.int32)
    places = ((core ^ (block % 2)) * 8 + (y_lo ^ (block // 8)) * 4 + (block // 2 % 4 - x + 4) % 4).astype(jnp.int32)

    blocks = normed_blocks(starts, inputs, gain)
    parts = [blocks[0], moved(blocks[3], z=-1), moved(blocks[2], z=2), moved(blocks[1], z=1)]
    *chunks, rows = grad_pre_of(after(places, *blocks), pre_gelu, grad_hidden)
    one = turned([after(parts[0], rows), *parts[1:]])
    columns = lax.all_gather(one, "tensor", axis=0, tiled=False)

    first = [moved(chunks[0], z=-1), moved(chunks[0], z=1)]

    own_right, *far_right = back(after(rows, one), w_in, 1)
    own_left, *far_left = back(after(rows, own_right), w_in, 0)
    own_right = after(own_right, own_left, *first)
    front, rear, next_right, last_right, own_right = added(
        add_right_kernel, [64, 64, 128, 128, 128], own_right, far_right
    )
    front, rear = moved(front, x=1), moved(rear, x=-1)
    keep, send = added(add_left_kernel, [256, 256], after(own_left, own_right), far_left)
    send = moved(send, y_lo=1)

    first_far = moved(after(first[1], own_right), z=1)
    second_next = moved(after(chunks[1], *first, own_right), z=-1)
    next_right = after(next_right, keep)
    ahead, behind = small(join_kernel, [like(128, 2560)] * 2, next_right, last_right, front, rear, lasts=1.2)
    second_far = moved(after(second_next, ahead), z=-1)
    second_last = moved(after(chunks[1], second_next, ahead, first_far), z=1)
    pieces = [[chunks[0], first[0], first_far, first[1]], [chunks[1], second_next, second_far, second_last]]
    ahead, behind = moved(ahead, x=1), moved(behind, x=-1)

    kept, *sent = weight("both", after(columns, second_next, ahead, behind), pieces[0])
    hop = [moved(sent[0], y=1), moved(sent[1], y=-1)]

    outs = [like(count, 2560) for count in (32, 32, 64, 64, 64)]
    keep = after(keep, *sent, second_far)
    front, rear, next_left, last_left, own_left = small(split_left_kernel, outs, keep, send)
    front, rear = moved(front, x=1), moved(rear, x=-1)

    sides = small(join_kernel, [like(64, 2560)] * 2, next_left, last_left, front, rear)
    kept_1, *sent = weight("both", after(columns, *sides), pieces[1])
    other = [moved(after(rows, kept_1), y=way) for rows, way in zip(hop, (1, -1))]
    right_keep, right_send = small(
        right_sum_kernel, [like(64, 2560, kind=F32), like(64, 2560)], after(own_right, *sent), ahead, behind
    )
    right_send = moved(right_send, y_lo=1)
    ahead, behind = moved(sides[0], x=1), moved(sides[1], x=-1)
    hop = [moved(sent[0], y=1), moved(sent[1], y=-1)]
    grad_w_in = put(after(kept, kept_1), *other, 2)
    (grad_in,) = small(
        end_kernel,
        [like(64, 5120)],
        inputs,
        gain,
        grad_out,
        after(own_left, grad_w_in),
        ahead,
        behind,
        right_keep,
        right_send,
        scratch=[pltpu.VMEM((64, 5120), F32)],
    )
    grad_w_in = put(after(kept_1, grad_in), moved(hop[0], y=1), moved(hop[1], y=-1), 0, [grad_w_in])
    return (grad_in, grad_w_in)


def solution(mesh):
    placed = (
        P(("dp", "tensor"), None),
        P(),
        P(None, "tensor"),
        P("dp", "tensor"),
        P("dp", "tensor"),
        P(("dp", "tensor"), None),
    )
    return jax.shard_map(
        local,
        mesh=mesh,
        in_specs=placed,
        out_specs=(P(("dp", "tensor"), None), P("dp", "tensor")),
        check_vma=False,
    )
```
